32 devices in a mesh: pair: 8 (over z, y), integral: 4 (over x, core).
Axes of the slice: x: 2, y: 2, z: 4, core: 2. Of those that a mesh axis runs over, the one named last changes fastest.
Arguments:
- occ_irrep: int32 [240], replicated, may hold values from 0 to 7
- amplitudes: bfloat16 [1920, 16384], P('pair', 'integral'), may hold values from -6 to 6
- ladder_ints: bfloat16 [16384, 16384], P('integral', 'pair'), may hold values from -0.046875 to 0.046875
- cycle_ints: bfloat16 [240, 128, 30720], P(None, 'integral', 'pair'), may hold values from -0.03125 to 0.03125
Outputs:
- residual: float32 [8, 240, 16384], P('integral', None, 'pair')
The draws below stay inside these ranges and needn't reach their ends.
Inputs may be any that keep to these rules, and one draw needn't show every extreme that they name: `occ_irrep`: irrep labels of D2h, below 8.
All inputs are finite; a program needn't handle non-finite values.
Results may differ from the reference program's by a relative error of at most 0.0003.
Values may be sent and summed in bfloat16 or wider, within the bound.
A program may use at most 256 MiB of HBM per device.

```python
import math
import jax
import jax.numpy as jnp
import numpy as np
from jax import lax

OCC = 240
VIRT = 128
IWIN = 8
OPAIRS = 1920


def touch_ends(drawn, own_key, least, largest):
    index_at = [jax.random.randint(jax.random.fold_in(own_key, axis), (), 0, length) for axis, length in enumerate(drawn.shape)]
    main_axis = drawn.shape.index(max(drawn.shape))
    beside = index_at[:main_axis] + [(index_at[main_axis] + 1) % drawn.shape[main_axis]] + index_at[main_axis + 1:]
    return drawn.at[tuple(index_at)].set(least).at[tuple(beside)].set(largest)


def steps_of(key, extent, pieces, least, high):
    gain = 1.0
    for position, parts in pieces:
        draws = jax.random.uniform(jax.random.fold_in(jax.random.fold_in(key, 6), position), (parts,), jnp.float32, least / len(pieces), high / len(pieces))
        gain = gain * jnp.repeat(jnp.exp(draws), extent[position] // parts).reshape((-1,) + (1,) * (len(extent) - 1 - position))
    return gain


def rank_bounds(amount, lean):
    loads = [(1 << 20) // math.isqrt(standing ** lean) + 1 for standing in range(1, amount + 1)]
    spread = 1 + sum(loads) // (1 << 30)
    return np.cumsum(np.array([max(1, weight // spread) for weight in loads]))


def ranked_ids(rng, extent, count, lean):
    listing = rank_bounds(count, lean)
    ticket = jax.random.randint(jax.random.fold_in(rng, 1), extent, 0, int(listing[count - 1]))
    standing = jnp.searchsorted(jnp.asarray(listing, jnp.int32), ticket, side="right")
    return jax.random.permutation(jax.random.fold_in(rng, 2), count)[standing].astype(jnp.int32)


def gaussian(rng, extent, spread, reach, pieces=(), held_as=jnp.bfloat16):
    level = steps_of(rng, extent, pieces, -0.22, 0.18) if pieces else 1.0
    drawn = jax.random.normal(rng, extent, jnp.float32) * spread * level
    return jnp.minimum(jnp.maximum(drawn, -reach), reach).astype(held_as)


def setup_inputs(seed: int = 0) -> dict:
    arg_keys = jax.random.split(jax.random.key(seed), 5)
    return {
        "occ_irrep": touch_ends(ranked_ids(arg_keys[0], (OCC,), 8, 4), jax.random.fold_in(arg_keys[0], 3), 0, 7).astype(jnp.int32),
        "amplitudes": gaussian(arg_keys[1], (OPAIRS, VIRT * VIRT), 1.0, 6.0, ((0, 8), (1, 4))),
        "ladder_ints": gaussian(arg_keys[2], (VIRT * VIRT, VIRT * VIRT), (VIRT * VIRT) ** -0.5, 0.046875, ((0, 4), (1, 8))),
        "cycle_ints": gaussian(arg_keys[3], (OCC, VIRT, VIRT * OCC), (OCC * VIRT) ** -0.5, 0.03125, ((1, 4), (2, 8))),
    }


def reference(occ_irrep, amplitudes, ladder_ints, cycle_ints):
    row_index = jnp.arange(IWIN * OCC, dtype=jnp.int32)
    pair_first = row_index // OCC
    pair_second = row_index % OCC
    allowed = occ_irrep[pair_first] == occ_irrep[pair_second]
    amp_sym = jnp.where(allowed[:, None], amplitudes, jnp.zeros((), amplitudes.dtype))
    ladder = jnp.dot(amp_sym, ladder_ints, preferred_element_type=jnp.float32).reshape(IWIN, OCC, VIRT * VIRT)
    cycle_flat = cycle_ints.reshape(OCC * VIRT, VIRT * OCC)

    def cycle_one(amp_one):
        return jnp.dot(amp_one.reshape(OCC * VIRT, VIRT).T, cycle_flat, preferred_element_type=jnp.float32)

    cycle_term = lax.map(cycle_one, amp_sym.reshape(IWIN, OCC * VIRT * VIRT)).reshape(IWIN, VIRT, VIRT, OCC)
    same_irrep = (occ_irrep[:IWIN][:, None] == occ_irrep[None, :]).astype(jnp.float32)
    cycle_term = cycle_term * same_irrep[:, None, None, :]
    cycle_moved = jnp.transpose(cycle_term, (0, 3, 1, 2)).reshape(IWIN, OCC, VIRT * VIRT)
    return ladder + cycle_moved
```

```python
import jax
import jax.numpy as jnp
from jax import lax
from jax.sharding import PartitionSpec as P

STEPS = 32767.0


def lookup_labels(indices, labels, occ_count):
    orbital = jnp.arange(occ_count, dtype=jnp.int32)
    return jnp.sum(jnp.where(indices[:, None] == orbital[None, :], labels[None, :], 0), axis=1)


def encode(values, axis):
    largest = jnp.max(jnp.abs(values), axis=axis, keepdims=True)
    unit = largest * (1.0 / STEPS)
    inverse = jnp.where(largest > 0, STEPS / jnp.where(largest > 0, largest, 1.0), 0.0)
    return jnp.round(values * inverse).astype(jnp.int32).astype(jnp.int16), unit


def decode(codes, unit):
    return codes.astype(jnp.int32).astype(jnp.float32) * unit


def reduce_blocks(partial, axis_name, parts):
    me = lax.axis_index(axis_name)
    blocks = partial.reshape((parts, partial.shape[0] // parts) + partial.shape[1:])
    left, bit = parts, 1
    while left > 1:
        own = (me // bit) % 2
        halves = blocks.reshape((left // 2, 2) + blocks.shape[1:])
        give = lax.dynamic_index_in_dim(halves, 1 - own, 1, keepdims=False)
        keep = lax.dynamic_index_in_dim(halves, own, 1, keepdims=False)
        swap = [(d, d ^ bit) for d in range(parts)]
        if bit == 1:
            got = lax.ppermute(give, axis_name, swap)
        else:
            codes, unit = encode(give, 2)
            got = decode(lax.ppermute(codes, axis_name, swap), lax.ppermute(unit, axis_name, swap))
        blocks = keep + got
        left, bit = left // 2, bit * 2
    return blocks[0]


def body(occ_irrep, amplitudes, ladder_ints, cycle_ints, *, pairs, parts):
    rows_local = amplitudes.shape[0]
    occ, vir_part, cycle_cols = cycle_ints.shape
    vir = amplitudes.shape[1] // vir_part
    vir_local = cycle_cols // occ
    window = rows_local * pairs // occ
    row_start = lax.axis_index("pair") * rows_local
    global_row = row_start + jnp.arange(rows_local, dtype=jnp.int32)
    allowed = lookup_labels(global_row // occ, occ_irrep, occ) == lookup_labels(global_row % occ, occ_irrep, occ)
    amp_sym = jnp.where(allowed[:, None], amplitudes, jnp.zeros((), amplitudes.dtype))

    per_orbital = occ // rows_local
    cut = (rows_local + 31) // 32 * 16
    cuts = [(0, cut), (cut, rows_local)]
    ints = cycle_ints.reshape(per_orbital, rows_local, vir_part, cycle_cols)
    cols_half = cycle_cols // 2
    sums = [None, None]
    ladders = []
    for number, (first, last) in enumerate(cuts):
        size = last - first
        gathered = lax.all_gather(amp_sym[first:last], "pair", axis=0, tiled=True)
        if number:
            gathered, sums[0], sums[1], ladders[0] = lax.optimization_barrier((gathered, sums[0], sums[1], ladders[0]))
        left = gathered.reshape(window, per_orbital * size * vir_part, vir)
        right = ints[:, first:last].reshape(per_orbital * size * vir_part, cycle_cols)
        ladder = jnp.dot(gathered, ladder_ints, preferred_element_type=jnp.float32)
        ladder = ladder.reshape(window, per_orbital * size, vir_local * vir)
        for half in range(2):
            term = jnp.einsum(
                "ixa,xn->ian", left, right[:, half * cols_half:(half + 1) * cols_half],
                preferred_element_type=jnp.float32,
            )
            sums[half] = term if number == 0 else sums[half] + term
        ladder = reduce_blocks(ladder, "integral", parts)
        ladders.append(ladder.reshape(window // parts, per_orbital, size, vir_local * vir))

    mine = window // parts
    a_local = vir // pairs
    cycles = []
    for half in range(2):
        cycle = reduce_blocks(sums[half], "integral", parts)
        codes, unit = encode(cycle, 2)
        codes = lax.all_to_all(codes.reshape(mine, pairs, a_local, cols_half), "pair", 1, 1, tiled=True)
        unit = lax.all_to_all(unit.reshape(mine, pairs, a_local, 1), "pair", 1, 1, tiled=True)
        cycles.append(decode(codes, unit).reshape(mine, pairs, a_local, vir_local // 2, occ))
    ladder = jnp.concatenate(ladders, axis=2).reshape(mine, occ, vir_local * vir)

    cycle = jnp.stack(cycles, axis=2)
    cycle = jnp.transpose(cycle, (0, 5, 3, 1, 2, 4)).reshape(mine, occ, a_local * vir)
    own = lax.axis_index("integral") * mine + jnp.arange(mine, dtype=jnp.int32)
    same = lookup_labels(own, occ_irrep, occ)[:, None] == occ_irrep[None, :]
    return ladder + cycle * same.astype(jnp.float32)[:, :, None]


def solution(mesh):
    placed = (P(), P("pair", "integral"), P("integral", "pair"), P(None, "integral", "pair"))

    def local(*arrays):
        return body(*arrays, pairs=mesh.shape["pair"], parts=mesh.shape["integral"])

    return jax.shard_map(
        local, mesh=mesh, in_specs=placed, out_specs=P("integral", None, "pair"), check_vma=False
    )
```
